32 devices in a mesh: grp: 4 (over x, core), seq: 8 (over z, y).
Axes of the slice: x: 2, y: 2, z: 4, core: 2. Of those that a mesh axis runs over, the one named last changes fastest.
Arguments:
- prompt_hidden: bfloat16 [16384, 7168], P(('grp', 'seq')), may hold values from -6 to 6
- decode_hidden: bfloat16 [2, 256, 7168], P(None, 'grp', 'seq'), may hold values from -6 to 6
- w_down: bfloat16 [7168, 2112], P('seq'), may hold values from -0.0625 to 0.0625
- kv_gain: float32 [512], replicated, may hold values from 0.1 to 1.9
- q_gain: float32 [1536], replicated, may hold values from 0.1 to 1.9
- w_uq: bfloat16 [1536, 12288], P(None, 'seq'), may hold values from -0.15625 to 0.15625
- w_uk: bfloat16 [64, 128, 512], P('seq'), may hold values from -0.5 to 0.5
- w_uv: bfloat16 [64, 512, 128], P('seq'), may hold values from -0.25 to 0.25
- w_out: bfloat16 [8192, 7168], P('seq'), may hold values from -0.09375 to 0.09375
- cache_lat: bfloat16 [256, 64, 576], P('grp')
- cache_len: int32 [256], replicated, may hold values from 2 to 64, as said below
- prompt_route: int32 [4], replicated, may hold values from 0 to 3, as said below
- row_slot: int32 [4, 4096], replicated, may hold values from 0 to 4095, as said below
Outputs:
- decoded: bfloat16 [2, 256, 7168], P(None, 'grp', 'seq')
The draws below stay inside these ranges and needn't reach their ends.
Inputs may be any that keep to these rules, and one draw needn't show every extreme that they name: `prompt_route`: a permutation: each decode group receives exactly one prefill group. Each row row_slot[g] is a permutation of 0 to 4095 that moves aligned pages of 8 rows whole, keeping the order inside a page. `cache_len`: every decode group has a sequence with 64 live rows.
All inputs are finite; a program needn't handle non-finite values.
Results may differ from the reference program's by a relative error of at most 0.025.
The reference program's roundings to bfloat16 on the way count: a program that leaves them out, or rounds other values in their place, can miss the bound.
Values may be sent and summed in bfloat16 or wider, within the bound.
No kernel may reach another device: no remote copies, remote signals or barrier semaphores. Data moves between devices by JAX's collectives and lax.ppermute only.
A program may use at most 128 MiB of HBM per device.

```python
import math
import jax
import jax.numpy as jnp
from jax import lax

D = 7168
QL = 1536
KVL = 512
ROPE = 64
NOPE = 128
VH = 128
HEADS = 64
BLOCK = 4096
BATCH = 64
EXT = 64
PAGE = 8
CACHE = 64
N_GRP = 4


def draw_prompt_route(key, part):
    key = jax.random.fold_in(key, 11)
    return jax.random.permutation(key, N_GRP).astype(jnp.int32)


def page_order(subkey):
    return jax.random.permutation(subkey, BLOCK // PAGE)


def draw_row_slot(key, part):
    key = jax.random.fold_in(key, 12)
    subkeys = jax.random.split(key, N_GRP)
    orders = jax.vmap(page_order)(subkeys).astype(jnp.int32)
    offsets = jnp.arange(BLOCK, dtype=jnp.int32)
    return (orders[:, offsets // PAGE] * PAGE + offsets % PAGE).astype(jnp.int32)


def draw_cache_len(key, part):
    key = jax.random.fold_in(key, 13)
    key_one, key_two, key_three = jax.random.split(key, 3)
    factor = jax.random.randint(key_one, (N_GRP, 1), 1, 5)
    base = jax.random.randint(key_two, (N_GRP, BATCH), 2, CACHE + 1)
    lengths = jnp.maximum(base * factor // 4, 2)
    longest = jax.random.randint(key_three, (N_GRP, 1), 0, BATCH)
    lengths = jnp.where(jnp.arange(BATCH)[None, :] == longest, CACHE, lengths)
    return lengths.reshape(-1).astype(jnp.int32)


def draw_cache_lat(key, part):
    key = jax.random.fold_in(key, 14)
    key_one = jax.random.fold_in(key, 0)
    shape = (N_GRP * BATCH, CACHE, KVL + ROPE)
    return jax.random.normal(key_one, shape, jnp.float32).astype(jnp.bfloat16)


def spiked(entries, stream_key, source, target, blocks, factor):
    owner, partner = [(jnp.arange(entries.shape[position]) // (entries.shape[position] // blocks)).reshape([-1 if axis == position else 1 for axis in range(entries.ndim)]) for position in (source, target)]
    chosen = jax.random.permutation(stream_key, blocks)[partner]
    strong = (owner == chosen) | (owner == (partner + blocks // 2) % blocks)
    return jnp.where(strong, factor * entries, entries)


def steps_of(own_key, extent, pieces, least, largest):
    level, own = 1.0, jax.random.fold_in(own_key, 6)
    for dim, shards_of in pieces:
        draws = jnp.exp(jax.random.uniform(jax.random.fold_in(own, dim), (shards_of,), jnp.float32, least / len(pieces), largest / len(pieces)))
        level = level * jnp.repeat(draws, extent[dim] // shards_of).reshape([-1 if axis == dim else 1 for axis in range(len(extent))])
    return level


def normal_values(stream_key, extent, deviation, most, shards=(), kind=jnp.bfloat16):
    values = deviation * jax.random.normal(stream_key, extent, jnp.float32)
    if shards:
        values = values * steps_of(stream_key, extent, shards, -0.22, 0.18)
    return jnp.clip(values, -most, most).astype(kind)


def gaussian_with(key, shape, spread, bound, cuts, heavy, held_as=jnp.bfloat16):
    entries = spread * jax.random.normal(key, shape, jnp.float32)
    if cuts:
        entries = entries * steps_of(key, shape, cuts, -0.22, 0.18)
    return jnp.clip(spiked(entries, jax.random.fold_in(key, 3), *heavy), -bound, bound).astype(held_as)


def setup_inputs(seed: int = 0) -> dict:
    key_of = jax.random.split(jax.random.key(seed), 14)
    return {
        "prompt_hidden": normal_values(key_of[0], (N_GRP * BLOCK, D), 1.0, 6.0, ((0, 32),)),
        "decode_hidden": normal_values(key_of[1], (2, N_GRP * BATCH, D), 1.0, 6.0, ((1, 4), (2, 8))),
        "w_down": normal_values(key_of[2], (D, QL + KVL + ROPE), D ** -0.5, 0.0625, ((0, 8),)),
        "kv_gain": jnp.clip(1.0 + 0.18 * jax.random.normal(key_of[3], (KVL,), jnp.float32), 0.1, 1.9),
        "q_gain": jnp.clip(1.0 + 0.18 * jax.random.normal(key_of[4], (QL,), jnp.float32), 0.1, 1.9),
        "w_uq": normal_values(key_of[5], (QL, HEADS * (NOPE + ROPE)), QL ** -0.5, 0.15625, ((1, 8),)),
        "w_uk": normal_values(key_of[6], (HEADS, NOPE, KVL), NOPE ** -0.5, 0.5, ((0, 8),)),
        "w_uv": normal_values(key_of[7], (HEADS, KVL, VH), KVL ** -0.5, 0.25, ((0, 8),)),
        "w_out": gaussian_with(key_of[8], (HEADS * VH, D), (HEADS * VH) ** -0.5, 0.09375, ((0, 8),), (0, 1, 8, 2.0)),
        "cache_lat": draw_cache_lat(jax.random.fold_in(key_of[13], 71), 0),
        "cache_len": draw_cache_len(jax.random.fold_in(key_of[13], 71), 0),
        "prompt_route": draw_prompt_route(jax.random.fold_in(key_of[13], 71), 0),
        "row_slot": draw_row_slot(jax.random.fold_in(key_of[13], 71), 0),
    }


def rms_norm(values, gain):
    return values * lax.rsqrt(lax.optimization_barrier(jnp.mean(values * values, axis=-1, keepdims=True)) + 1e-06) * gain

def rotate_half(values, positions):
    half = values.shape[-1] // 2
    ladder = jnp.arange(half, dtype=jnp.float32)
    freq = jnp.exp(ladder * (-2.0 * math.log(10000.0) / values.shape[-1]))
    angle = positions.astype(jnp.float32)[..., None] * freq
    cosine = jnp.cos(angle)
    sine = jnp.sin(angle)
    first_half = values[..., :half]
    second_half = values[..., half:]
    return jnp.concatenate([first_half * cosine - second_half * sine, second_half * cosine + first_half * sine], axis=-1)

def make_key(latent, gain, positions):
    width = gain.shape[0]
    normed = rms_norm(latent[..., :width], gain)
    turned = rotate_half(latent[..., width:], positions)
    return jnp.concatenate([normed, turned], axis=-1).astype(jnp.bfloat16)

def reference(prompt_hidden, decode_hidden, w_down, kv_gain, q_gain, w_uq, w_uk, w_uv, w_out, cache_lat, cache_len, prompt_route, row_slot):
    kv_weight = w_down[:, QL:]
    prompts = prompt_hidden.reshape(N_GRP, BLOCK, D)
    group_lens = cache_len.reshape(N_GRP, BATCH)

    def prefill(inputs):
        tokens_here, slots_here, route_here = inputs
        lens_here = group_lens[route_here]
        positions = (lens_here[slots_here // EXT] + slots_here % EXT).astype(jnp.int32)
        latent = jnp.dot(tokens_here, kv_weight, preferred_element_type=jnp.float32)
        new_rows = make_key(latent, kv_gain, positions)
        return jnp.zeros((BLOCK, KVL + ROPE), jnp.bfloat16).at[slots_here].set(new_rows)
    placed = lax.map(prefill, (prompts, row_slot, prompt_route))
    arrival = jnp.zeros_like(placed).at[prompt_route].set(placed).reshape(N_GRP * BATCH, EXT, KVL + ROPE)
    seq_total = N_GRP * BATCH
    down = jnp.dot(decode_hidden.reshape(2 * seq_total, D), w_down, preferred_element_type=jnp.float32).reshape(2, seq_total, -1)
    step_index = jnp.arange(2, dtype=jnp.int32)
    dec_positions = cache_len[None, :] + EXT + step_index[:, None]
    q_latent = rms_norm(down[..., :QL], q_gain).astype(jnp.bfloat16)
    fresh = make_key(down[..., QL:], kv_gain, dec_positions)
    projected = jnp.dot(q_latent.reshape(2 * seq_total, QL), w_uq, preferred_element_type=jnp.float32)
    projected = projected.astype(jnp.bfloat16).reshape(2, seq_total, HEADS, NOPE + ROPE)
    absorbed = jnp.einsum('trhn,hnc->trhc', projected[..., :NOPE].astype(jnp.float32), w_uk.astype(jnp.float32))
    rotated = rotate_half(projected[..., NOPE:].astype(jnp.float32), dec_positions[..., None])
    queries = jnp.concatenate([absorbed, rotated], axis=-1).astype(jnp.bfloat16)
    key_rows = jnp.concatenate([cache_lat, arrival, jnp.transpose(fresh, (1, 0, 2))], axis=1)
    key_total = CACHE + EXT + 2
    key_index = jnp.arange(key_total, dtype=jnp.int32)
    in_cache = key_index[None, None, :] < cache_len[None, :, None]
    visible = jnp.where((key_index < CACHE)[None, None, :], in_cache, jnp.where((key_index == key_total - 1)[None, None, :], step_index[:, None, None] == 1, True))
    scores = jnp.einsum('trhc,rkc->trhk', queries.astype(jnp.float32), key_rows.astype(jnp.float32)) * (NOPE + ROPE) ** (-0.5)
    scores = jnp.where(visible[:, :, None, :], scores, -1e+30)
    highest = lax.optimization_barrier(jnp.max(scores, axis=-1, keepdims=True))
    expo = jnp.exp(scores - highest)
    probs = (expo / lax.optimization_barrier(jnp.sum(expo, axis=-1, keepdims=True))).astype(jnp.bfloat16)
    context = jnp.einsum('trhk,rkc->trhc', probs.astype(jnp.float32), key_rows[..., :KVL].astype(jnp.float32)).astype(jnp.bfloat16)
    head_out = jnp.einsum('trhc,hcv->trhv', context.astype(jnp.float32), w_uv.astype(jnp.float32)).astype(jnp.bfloat16)
    decoded = jnp.dot(head_out.reshape(2 * seq_total, HEADS * VH), w_out, preferred_element_type=jnp.float32)
    return decoded.astype(jnp.bfloat16).reshape(2, seq_total, D)
```

```python
import math

import jax
import jax.numpy as jnp
from jax import lax
from jax.sharding import PartitionSpec as P


def ring_order(count):
    if count == 16:
        cells = [(0, 0), (0, 1), (0, 2), (0, 3), (1, 3), (1, 2), (1, 1), (2, 1)]
        cells += [(2, 2), (2, 3), (3, 3), (3, 2), (3, 1), (3, 0), (2, 0), (1, 0)]
        return [a * 4 + b for a, b in cells]
    return list(range(0, count, 2)) + list(range(count - 1, 0, -2))


def rms_norm(values, gain):
    return values * lax.rsqrt(jnp.mean(values * values, axis=-1, keepdims=True) + 1e-06) * gain


def rotate_half(values, positions):
    half = values.shape[-1] // 2
    ladder = jnp.arange(half, dtype=jnp.float32)
    freq = jnp.exp(ladder * (-2.0 * math.log(10000.0) / values.shape[-1]))
    angle = positions.astype(jnp.float32)[..., None] * freq
    cosine = jnp.cos(angle)
    sine = jnp.sin(angle)
    first_half = values[..., :half]
    second_half = values[..., half:]
    return jnp.concatenate(
        [first_half * cosine - second_half * sine, second_half * cosine + first_half * sine],
        axis=-1,
    )


def make_key(latent, gain, positions):
    width = gain.shape[0]
    normed = rms_norm(latent[..., :width], gain)
    turned = rotate_half(latent[..., width:], positions)
    return jnp.concatenate([normed, turned], axis=-1).astype(jnp.bfloat16)


class Ring:
    def __init__(self, count):
        self.count = count
        self.order = ring_order(count)
        places = [0] * count
        for place, index in enumerate(self.order):
            places[index] = place
        self.place = jnp.array(places, jnp.int32)[lax.axis_index("seq")]
        nexts = self.order[1:] + self.order[:1]
        self.forward = list(zip(self.order, nexts))
        self.backward = [(b, a) for a, b in self.forward]

    def member(self, offset):
        return jnp.array(self.order, jnp.int32)[(self.place + offset) % self.count]

    def send(self, value, forward):
        return lax.ppermute(value, "seq", self.forward if forward else self.backward)

    def gather(self, block):
        half = self.count // 2
        ahead = behind = block
        for step in range(1, half):
            ahead = self.send(ahead, True)
            behind = self.send(behind, False)
            yield self.member(-step), 0, ahead
            yield self.member(step), 0, behind
        cut = block.shape[0] // 2
        last_ahead = self.send(ahead[:cut], True)
        last_behind = self.send(behind[cut:], False)
        yield self.member(half), 0, last_ahead
        yield self.member(half), cut, last_behind

    def reduce_scatter(self, part_of, columns):
        half = self.count // 2
        cut = columns // 2
        far = part_of(self.member(half))
        ahead = self.send(far[:, :cut].astype(jnp.bfloat16), True)
        behind = self.send(far[:, cut:].astype(jnp.bfloat16), False)
        for step in range(half - 1, 0, -1):
            near_ahead = part_of(self.member(step))
            near_behind = part_of(self.member(-step))
            if step == half - 1:
                near_ahead = jnp.concatenate(
                    [near_ahead[:, :cut] + ahead.astype(jnp.float32), near_ahead[:, cut:]], axis=1
                )
                near_behind = jnp.concatenate(
                    [near_behind[:, :cut], near_behind[:, cut:] + behind.astype(jnp.float32)],
                    axis=1,
                )
            else:
                near_ahead = near_ahead + ahead.astype(jnp.float32)
                near_behind = near_behind + behind.astype(jnp.float32)
            ahead = self.send(near_ahead.astype(jnp.bfloat16), True)
            behind = self.send(near_behind.astype(jnp.bfloat16), False)
        own = part_of(self.member(0))
        return own + (ahead.astype(jnp.float32) + behind.astype(jnp.float32))


def local(
    prompt_hidden,
    decode_hidden,
    w_down,
    kv_gain,
    q_gain,
    w_uq,
    w_uk,
    w_uv,
    w_out,
    cache_lat,
    cache_len,
    prompt_route,
    row_slot,
):
    seq_count = lax.axis_size("seq")
    group_count = lax.axis_size("grp")
    seq_index = lax.axis_index("seq")
    group_index = lax.axis_index("grp")
    token_count = prompt_hidden.shape[0]
    width_share = w_down.shape[0]
    q_width = q_gain.shape[0]
    kv_width = kv_gain.shape[0]
    latent_width = w_down.shape[1] - q_width
    batch = cache_lat.shape[0]
    block_total = token_count * seq_count
    extra = block_total // batch
    steps = decode_hidden.shape[0]
    core = group_index % 2
    chip = group_index // 2
    chips = group_count // 2
    ring = Ring(seq_count)
    swap_cores = [(g, g ^ 1) for g in range(group_count)]

    kv_weight = w_down[:, q_width:]
    share = width_share // 2
    carried = lax.dynamic_slice_in_dim(kv_weight, core * share, share, 0)
    weight = jnp.zeros((width_share * seq_count, latent_width), jnp.bfloat16)
    weight = lax.dynamic_update_slice_in_dim(weight, kv_weight, seq_index * width_share, 0)
    for member, start, rows in ring.gather(carried):
        swapped = lax.ppermute(rows, "grp", swap_cores)
        base = member * width_share + start
        weight = lax.dynamic_update_slice_in_dim(weight, rows, base + core * share, 0)
        weight = lax.dynamic_update_slice_in_dim(weight, swapped, base + (1 - core) * share, 0)

    decode_rows = steps * batch
    flat_hidden = decode_hidden.reshape(decode_rows, width_share)
    partial_down = jnp.dot(flat_hidden, w_down, preferred_element_type=jnp.float32)
    down = lax.psum_scatter(partial_down, "seq", scatter_dimension=0, tiled=True)
    local_len = lax.dynamic_slice_in_dim(cache_len, group_index * batch, batch, 0)
    own_rows = decode_rows // seq_count
    own_index = seq_index * own_rows + jnp.arange(own_rows, dtype=jnp.int32)
    own_positions = local_len[own_index % batch] + extra + own_index // batch
    own_latent = jnp.concatenate(
        [
            rms_norm(down[:, :q_width], q_gain).astype(jnp.bfloat16),
            make_key(down[:, q_width:], kv_gain, own_positions),
        ],
        axis=1,
    )
    latents = lax.all_gather(own_latent, "seq", axis=0, tiled=True)
    q_latent = latents[:, :q_width]
    fresh = latents[:, q_width:].reshape(steps, batch, latent_width)

    target = prompt_route[group_index]
    target_lens = lax.dynamic_slice_in_dim(cache_len, target * batch, batch, 0)
    own_slots = lax.dynamic_slice_in_dim(
        lax.dynamic_index_in_dim(row_slot, group_index, 0, keepdims=False),
        seq_index * token_count,
        token_count,
        0,
    )
    owner_len = jnp.sum(
        jnp.where(
            (own_slots // extra)[:, None] == jnp.arange(batch, dtype=jnp.int32)[None, :],
            target_lens[None, :],
            0,
        ),
        axis=1,
    )
    positions = owner_len + own_slots % extra
    latent = jnp.dot(prompt_hidden, weight, preferred_element_type=jnp.float32)
    new_rows = make_key(latent, kv_gain, positions)

    groups = jnp.arange(group_count, dtype=jnp.int32)
    sources = jnp.sum(
        jnp.where(prompt_route[None, :] == groups[:, None], groups[None, :], 0), axis=1
    )
    source = sources[group_index]
    other_rows = lax.ppermute(new_rows, "grp", swap_cores)
    chosen = jnp.where(source % 2 == core, new_rows, other_rows)
    for shift in range(1, chips):
        reached = sources[((chip + shift) % chips) * 2 + core]
        outgoing = jnp.where(reached % 2 == core, new_rows, other_rows)
        incoming = lax.ppermute(
            outgoing, "grp", [(g, (g + 2 * shift) % group_count) for g in range(group_count)]
        )
        chosen = jnp.where(source // 2 == (chip - shift) % chips, incoming, chosen)
    block_rows = jnp.zeros((block_total, latent_width), jnp.bfloat16)
    block_rows = lax.dynamic_update_slice_in_dim(block_rows, chosen, seq_index * token_count, 0)
    for member, start, rows in ring.gather(chosen):
        block_rows = lax.dynamic_update_slice_in_dim(
            block_rows, rows, member * token_count + start, 0
        )

    page = 8
    slots = lax.dynamic_index_in_dim(row_slot, source, 0, keepdims=False)
    page_of = slots.reshape(-1, page)[:, 0] // page
    pages = page_of.shape[0]
    page_index = jnp.arange(pages, dtype=jnp.int32)
    page_from = jnp.sum(
        jnp.where(page_of[None, :] == page_index[:, None], page_index[None, :], 0), axis=1
    )
    arrival = block_rows.reshape(pages, page, latent_width)[page_from].reshape(
        batch, extra, latent_width
    )

    step_index = jnp.arange(steps, dtype=jnp.int32)
    dec_positions = local_len[None, :] + extra + step_index[:, None]
    head_count = w_uk.shape[0]
    nope_width = w_uk.shape[1]
    rope_width = latent_width - kv_width
    projected = jnp.dot(q_latent, w_uq, preferred_element_type=jnp.float32)
    projected = projected.astype(jnp.bfloat16).reshape(
        steps, batch, head_count, nope_width + rope_width
    )
    absorbed = jnp.einsum(
        "tbhn,hnc->tbhc", projected[..., :nope_width], w_uk, preferred_element_type=jnp.float32
    )
    rotated = rotate_half(projected[..., nope_width:].astype(jnp.float32), dec_positions[..., None])
    queries = jnp.concatenate([absorbed, rotated], axis=-1).astype(jnp.bfloat16)
    key_rows = jnp.concatenate([cache_lat, arrival, jnp.transpose(fresh, (1, 0, 2))], axis=1)
    cache_size = cache_lat.shape[1]
    key_total = key_rows.shape[1]
    key_index = jnp.arange(key_total, dtype=jnp.int32)
    in_cache = key_index[None, None, :] < local_len[None, :, None]
    visible = jnp.where(
        (key_index < cache_size)[None, None, :],
        in_cache,
        jnp.where(
            (key_index == key_total - 1)[None, None, :], step_index[:, None, None] == 1, True
        ),
    )
    scores = jnp.einsum("tbhc,bkc->tbhk", queries, key_rows, preferred_element_type=jnp.float32) * (
        nope_width + rope_width
    ) ** (-0.5)
    scores = jnp.where(visible[:, :, None, :], scores, -1e30)
    highest = jnp.max(scores, axis=-1, keepdims=True)
    expo = jnp.exp(scores - highest)
    probs = (expo / jnp.sum(expo, axis=-1, keepdims=True)).astype(jnp.bfloat16)
    context = jnp.einsum(
        "tbhk,bkc->tbhc", probs, key_rows[..., :kv_width], preferred_element_type=jnp.float32
    ).astype(jnp.bfloat16)
    head_out = jnp.einsum(
        "tbhc,hcv->tbhv", context, w_uv, preferred_element_type=jnp.float32
    ).astype(jnp.bfloat16)
    head_out = head_out.reshape(decode_rows, -1)
    feature_share = w_out.shape[1] // seq_count

    def part_of(member):
        columns = lax.dynamic_slice_in_dim(w_out, member * feature_share, feature_share, 1)
        return jnp.dot(head_out, columns, preferred_element_type=jnp.float32)

    total = ring.reduce_scatter(part_of, feature_share)
    return total.reshape(steps, batch, feature_share).astype(jnp.bfloat16)


def solution(mesh):
    in_specs = (
        P(("grp", "seq"), None),
        P(None, "grp", "seq"),
        P("seq", None),
        P(),
        P(),
        P(None, "seq"),
        P("seq", None, None),
        P("seq", None, None),
        P("seq", None),
        P("grp", None, None),
        P(),
        P(),
        P(),
    )
    out_specs = P(None, "grp", "seq")
    return jax.shard_map(local, mesh=mesh, in_specs=in_specs, out_specs=out_specs, check_vma=False)
```
